32 devices in a mesh: parts: 2 (over y), chain: 4 (over x, core), group: 4 (over z).
Axes of the slice: x: 2, y: 2, z: 4, core: 2. Of those that a mesh axis runs over, the one named last changes fastest.
Arguments:
- rhs: float32 [8, 5, 64, 64], P(('parts', 'chain'), None, None, 'group'), parts along dimension 0, may hold values from -6 to 6
- inv_block: float32 [8, 64, 320, 320], P(('parts', 'chain'), 'group'), parts along dimension 0, may hold values from -0.3125 to 0.3125
- flux_jac: float32 [8, 3, 5, 5, 64], P(('parts', 'chain'), None, None, None, 'group'), parts along dimension 0, may hold values from -2.5 to 2.5
- up_elem: int32 [8, 3, 64], P(('parts', 'chain'), None, 'group'), parts along dimension 0, may hold values from 0 to 63, each once within a row
- lift: float32 [3, 64, 16], replicated, may hold values from -0.875 to 0.875
Outputs:
- solution: float32 [8, 5, 64, 64], P(('parts', 'chain'), None, None, 'group'), parts along dimension 0
The draws below stay inside these ranges and needn't reach their ends.
There are 2 independent parts, one for each index of `parts`. The reference program is written for one: setup_inputs(seed, part) draws one part's arguments, and reference() takes and returns one part's arrays. A program takes and returns all parts, laid end to end along the dimension named above; an argument that names none is the same for every part. Nothing has to cross between parts.
Inputs may be any that keep to these rules, and one draw needn't show every extreme that they name: For every section s and face k, up_elem[s, k, :] names each of the 64 elements once; row s = 0 is not read.
All inputs are finite; a program needn't handle non-finite values.
Results may differ from the reference program's by a relative error of at most 0.02.
Values may be sent and summed in bfloat16 or wider, within the bound.
A program may use at most 64 MiB of HBM per device.

```python
import jax
import jax.numpy as jnp
from jax import lax

VARS = 5
NP = 4
NODES = 64
FACE = 16
BLOCK = 320
S_TOTAL = 4
E_SECTION = 64


def block_levels(stream_key, shape, cuts, smallest, top_value):
    gain = 1.0
    for axis_at, blocks in cuts:
        draws = jax.random.uniform(jax.random.fold_in(jax.random.fold_in(stream_key, 6), axis_at), (blocks,), jnp.float32, smallest / len(cuts), top_value / len(cuts))
        gain = gain * jnp.repeat(jnp.exp(draws), shape[axis_at] // blocks).reshape((-1,) + (1,) * (len(shape) - 1 - axis_at))
    return gain


def noise(rng, shape, spread, most, split=(), held_as=jnp.bfloat16):
    entries = spread * jax.random.normal(rng, shape, jnp.float32)
    if split:
        entries = entries * block_levels(rng, shape, split, -0.22, 0.18)
    return jnp.clip(entries, -most, most).astype(held_as)


def setup_inputs(seed: int = 0, part: int = 0) -> dict:
    streams_of = jax.random.split(jax.random.key(seed), 6)
    part_splits = jax.random.split(jax.random.fold_in(streams_of[5], part), 6)
    return {
        "rhs": noise(part_splits[0], (S_TOTAL, VARS, NODES, E_SECTION), 1.0, 6.0, ((0, 4), (3, 4)), jnp.float32),
        "inv_block": noise(part_splits[1], (S_TOTAL, E_SECTION, BLOCK, BLOCK), BLOCK ** -0.5, 0.3125, ((0, 4), (1, 4)), jnp.float32),
        "flux_jac": noise(part_splits[2], (S_TOTAL, 3, VARS, VARS, E_SECTION), (VARS + 1) ** -0.5, 2.5, ((0, 4), (4, 4)), jnp.float32),
        "up_elem": jax.vmap(lambda own: jax.random.permutation(own, E_SECTION))(jax.random.split(part_splits[3], S_TOTAL * 3)).reshape((S_TOTAL, 3, E_SECTION)).astype(jnp.int32),
        "lift": noise(streams_of[4], (3, NODES, FACE), (3 * FACE) ** -0.5, 0.875, (), jnp.float32),
    }


HIGH = lax.Precision.HIGHEST


def face_traces(solved):
    elements = solved.shape[-1]
    cube = solved.reshape(VARS, NP, NP, NP, elements)
    first = cube[:, NP - 1, :, :, :].reshape(VARS, FACE, elements)
    second = cube[:, :, NP - 1, :, :].reshape(VARS, FACE, elements)
    third = cube[:, :, :, NP - 1, :].reshape(VARS, FACE, elements)
    return jnp.stack([first, second, third]).astype(jnp.bfloat16)


def solve_section(rhs_s, inv_s, jac_s, up_s, prev_full, lift):
    elements = rhs_s.shape[-1]
    picked = jnp.stack([jnp.take(prev_full[k], up_s[k].astype(jnp.int32), axis=2) for k in range(3)])
    upstream = picked.astype(jnp.float32)
    mixed = jnp.einsum("kwve,kvfe->kwfe", jac_s, upstream, precision=HIGH)
    coupling = jnp.einsum("kif,kwfe->wie", lift, mixed, precision=HIGH)
    flat = (rhs_s - coupling).reshape(VARS * NODES, elements)
    result = jnp.einsum("eij,je->ie", inv_s, flat, precision=HIGH)
    return result.reshape(VARS, NODES, elements)


def reference(rhs, inv_block, flux_jac, up_elem, lift):
    start = jnp.zeros((3, VARS, FACE, E_SECTION), jnp.bfloat16)

    def section_step(prev_full, items):
        rhs_s, inv_s, jac_s, up_s = items
        solved = solve_section(rhs_s, inv_s, jac_s, up_s, prev_full, lift)
        return face_traces(solved), solved

    final, solution = lax.scan(section_step, start, (rhs, inv_block, flux_jac, up_elem))
    return solution
```

```python
import functools

import jax
import jax.numpy as jnp
from jax import lax
from jax.experimental import pallas as pl
from jax.experimental.pallas import tpu as pltpu
from jax.sharding import PartitionSpec as P

VARS = 5
NODES = 64
FACE = 16
BLOCK = VARS * NODES
FACES = 3
LANES = 128
WIDE = FACES * LANES
SHIFTS = tuple(range(1 - VARS, VARS))
MESH = pl.DeviceIdType.MESH
F32 = jnp.float32
BF16 = jnp.bfloat16


def iota(shape, axis):
    return lax.broadcasted_iota(jnp.int32, shape, axis)


def select_operator(k):
    col = iota((BLOCK, LANES), 1)
    f = col & 15
    if k == 0:
        node = 48 + f
    elif k == 1:
        node = ((f >> 2) << 4) + 12 + (f & 3)
    else:
        node = (f << 2) + 3
    wanted = ((col >> 4) << 6) + node
    return jnp.where(iota((BLOCK, LANES), 0) == wanted, 1.0, 0.0).astype(BF16)


def kernel(chains, groups, local, rhs_hbm, inv_hbm, jac_hbm, up_hbm, lift_hbm, out_hbm,
           rhs_v, inv_v, jac_v, up_v, lift_v, out_v, invb, sel, liftb, mix, hot, res, outgoing, incoming,
           small_sem, inv_sem, out_sem, send_sem, recv_sem):
    s = lax.axis_index("chain")
    g = lax.axis_index("group")
    small = [
        pltpu.make_async_copy(src, dst, small_sem.at[n])
        for n, (src, dst) in enumerate(
            ((up_hbm.at[0], up_v), (jac_hbm.at[0], jac_v), (lift_hbm, lift_v), (rhs_hbm.at[0], rhs_v))
        )
    ]
    for copy in small:
        copy.start()
    blocks = [pltpu.make_async_copy(inv_hbm.at[0, e], inv_v.at[e], inv_sem.at[e]) for e in range(local)]
    for copy in blocks:
        copy.start()

    barrier = pltpu.get_barrier_semaphore()

    @pl.when(s > 0)
    def _():
        for other in range(groups):
            pl.semaphore_signal(
                barrier, inc=1, device_id={"chain": s - 1, "group": other}, device_id_type=MESH
            )

    for k in range(FACES):
        sel[:, k * LANES:(k + 1) * LANES] = select_operator(k)

    for copy in small:
        copy.wait()

    res[...] = jnp.transpose(rhs_v[...].reshape(BLOCK, local))

    @pl.when(s > 0)
    def _():
        elements = groups * local
        slot = iota((local, LANES), 1) >> 4
        for k in range(FACES):
            match = jnp.where(iota((elements, local), 0) == up_v[k:k + 1, :], 1.0, 0.0)
            hot[k] = jnp.transpose(match).astype(BF16)
            part = jnp.transpose(lift_v[k])
            wide = jnp.concatenate([part] * VARS, axis=1)
            place = iota((FACE, BLOCK), 1) >> 6
            for w in range(VARS):
                liftb[k * LANES + w * FACE:k * LANES + (w + 1) * FACE, :] = jnp.where(
                    place == w, wide, 0.0
                ).astype(BF16)
            liftb[k * LANES + VARS * FACE:(k + 1) * LANES, :] = jnp.zeros(
                (LANES - VARS * FACE, BLOCK), BF16
            )
            columns = [jnp.transpose(jac_v[k, w]) for w in range(VARS)]
            for n, d in enumerate(SHIFTS):
                total = jnp.zeros((local, LANES), F32)
                for w in range(VARS):
                    if 0 <= w - d < VARS:
                        total = jnp.where(slot == w, columns[w][:, w - d:w - d + 1], total)
                mix[k, n] = total

    for e in range(local):
        blocks[e].wait()
        invb[e] = inv_v[e].astype(BF16)

    @pl.when(s > 0)
    def _():
        for other in range(groups):
            pltpu.make_async_remote_copy(
                src_ref=outgoing,
                dst_ref=incoming.at[pl.ds(other * local, local), :],
                send_sem=send_sem.at[other],
                recv_sem=recv_sem.at[other],
                device_id={"chain": s - 1, "group": other},
                device_id_type=MESH,
            ).wait_recv()
        mixed = []
        for k in range(FACES):
            u = jnp.dot(hot[k], incoming[:, k * LANES:(k + 1) * LANES], preferred_element_type=F32)
            total = jnp.zeros((local, LANES), F32)
            for n, d in enumerate(SHIFTS):
                moved = u if d == 0 else pltpu.roll(u, (d * FACE) % LANES, 1)
                total = total + moved * mix[k, n]
            mixed.append(total.astype(BF16))
        coupling = jnp.dot(jnp.concatenate(mixed, axis=1), liftb[...], preferred_element_type=F32)
        res[...] = res[...] - coupling

    given = res[...].astype(BF16)
    row = iota((local, BLOCK), 0)
    solved = jnp.zeros((local, BLOCK), F32)
    for e in range(local):
        one = lax.dot_general(given, invb[e], (((1,), (1,)), ((), ())), preferred_element_type=F32)
        solved = jnp.where(row == e, one, solved)
    traces = jnp.dot(solved.astype(BF16), sel[...], preferred_element_type=F32)
    outgoing[...] = traces.astype(BF16)

    def sends():
        return [
            pltpu.make_async_remote_copy(
                src_ref=outgoing,
                dst_ref=incoming.at[pl.ds(pl.multiple_of(g * local, local), local), :],
                send_sem=send_sem.at[other],
                recv_sem=recv_sem.at[g],
                device_id={"chain": s + 1, "group": other},
                device_id_type=MESH,
            )
            for other in range(groups)
        ]

    @pl.when(s < chains - 1)
    def _():
        pl.semaphore_wait(barrier, groups)
        for copy in sends():
            copy.start()

    out_v[...] = jnp.transpose(solved).reshape(VARS, NODES, local)
    result = pltpu.make_async_copy(out_v, out_hbm.at[0], out_sem)
    result.start()

    @pl.when(s < chains - 1)
    def _():
        for copy in sends():
            copy.wait_send()

    result.wait()


def body(chains, groups, rhs, inv_block, flux_jac, up_elem, lift):
    local = rhs.shape[3]
    elements = groups * local
    anywhere = pl.BlockSpec(memory_space=pl.ANY)
    return pl.pallas_call(
        functools.partial(kernel, chains, groups, local),
        out_shape=jax.ShapeDtypeStruct(rhs.shape, F32),
        in_specs=[anywhere] * 5,
        out_specs=anywhere,
        scratch_shapes=[
            pltpu.VMEM((VARS, NODES, local), F32),
            pltpu.VMEM((local, BLOCK, BLOCK), F32),
            pltpu.VMEM((FACES, VARS, VARS, local), F32),
            pltpu.VMEM((FACES, local), jnp.int32),
            pltpu.VMEM((FACES, NODES, FACE), F32),
            pltpu.VMEM((VARS, NODES, local), F32),
            pltpu.VMEM((local, BLOCK, BLOCK), BF16),
            pltpu.VMEM((BLOCK, WIDE), BF16),
            pltpu.VMEM((WIDE, BLOCK), BF16),
            pltpu.VMEM((FACES, len(SHIFTS), local, LANES), F32),
            pltpu.VMEM((FACES, local, elements), BF16),
            pltpu.VMEM((local, BLOCK), F32),
            pltpu.VMEM((local, WIDE), BF16),
            pltpu.VMEM((elements, WIDE), BF16),
            pltpu.SemaphoreType.DMA((4,)),
            pltpu.SemaphoreType.DMA((local,)),
            pltpu.SemaphoreType.DMA,
            pltpu.SemaphoreType.DMA((groups,)),
            pltpu.SemaphoreType.DMA((groups,)),
        ],
        compiler_params=pltpu.CompilerParams(
            collective_id=0, has_side_effects=True, vmem_limit_bytes=40 * 1024 * 1024
        ),
    )(rhs, inv_block, flux_jac, up_elem, lift)


def solution(mesh):
    return jax.shard_map(
        functools.partial(body, mesh.shape["chain"], mesh.shape["group"]),
        mesh=mesh,
        in_specs=(
            P(("parts", "chain"), None, None, "group"),
            P(("parts", "chain"), "group", None, None),
            P(("parts", "chain"), None, None, None, "group"),
            P(("parts", "chain"), None, "group"),
            P(),
        ),
        out_specs=P(("parts", "chain"), None, None, "group"),
        check_vma=False,
    )
```

```python
import functools

import jax
import jax.numpy as jnp
from jax import lax
from jax.experimental import pallas as pl
from jax.experimental.pallas import tpu as pltpu
from jax.sharding import PartitionSpec as P

VARS = 5
NODES = 64
FACE = 16
BLOCK = VARS * NODES
FACES = 3
SIDE = VARS * FACE
USED = FACES * SIDE
WIDE = 256
MESH = pl.DeviceIdType.MESH
F32 = jnp.float32
BF16 = jnp.bfloat16


def iota(shape, axis):
    return lax.broadcasted_iota(jnp.int32, shape, axis)


def select_operator():
    shape = (BLOCK, WIDE)
    col = iota(shape, 1)
    second, third = col >= SIDE, col >= 2 * SIDE
    rest = col - jnp.where(third, 2 * SIDE, jnp.where(second, SIDE, 0))
    f = rest & 15
    node = jnp.where(third, (f << 2) + 3, jnp.where(second, ((f >> 2) << 4) + 12 + (f & 3), 48 + f))
    wanted = jnp.where(col < USED, ((rest >> 4) << 6) + node, BLOCK)
    return jnp.where(iota(shape, 0) == wanted, 1.0, 0.0).astype(BF16)


def halves(x):
    high = x.astype(BF16)
    return high, (x - high.astype(F32)).astype(BF16)


def times_transposed(a, b):
    return lax.dot_general(a, b, (((1,), (1,)), ((), ())), preferred_element_type=F32)


def face_rows(block):
    rows = []
    cube = block[...]
    rows.append(cube.reshape(VARS, NODES, BLOCK)[:, NODES - FACE:, :].reshape(SIDE, BLOCK))
    rows.append(cube.reshape(VARS * 4, 16, BLOCK)[:, 12:, :].reshape(SIDE, BLOCK))
    rows.append(cube.reshape(SIDE, 4, BLOCK)[:, 3, :])
    return jnp.concatenate(rows, axis=0)


def kernel(chains, groups, local, rhs_hbm, inv_hbm, jac_hbm, up_hbm, lift_hbm, out_hbm,
           rhs_v, inv_v, jac_v, up_v, lift_v, out_v, sel, wide_lift, coeff, hot, given, base, base_t, full, short,
           outgoing, incoming, small_sem, inv_sem, out_sem, send_sem, recv_sem):
    s = lax.axis_index("chain")
    g = lax.axis_index("group")
    last = chains - 1
    small = [
        pltpu.make_async_copy(src, dst, small_sem.at[n])
        for n, (src, dst) in enumerate(
            ((up_hbm, up_v), (jac_hbm, jac_v), (lift_hbm, lift_v), (rhs_hbm.at[0], rhs_v))
        )
    ]
    for copy in small:
        copy.start()
    blocks = [pltpu.make_async_copy(inv_hbm.at[0, e], inv_v.at[e], inv_sem.at[e]) for e in range(local)]
    for copy in blocks:
        copy.start()

    barrier = pltpu.get_barrier_semaphore()

    @pl.when(s > 0)
    def _():
        for other in range(groups):
            pl.semaphore_signal(
                barrier, inc=1, device_id={"chain": s - 1, "group": other}, device_id_type=MESH
            )

    row = iota((local, BLOCK), 0)
    row_t = iota((local, WIDE), 0)
    sel[...] = select_operator()
    for copy in small:
        copy.wait()
    high, low = halves(jnp.concatenate([rhs_v[v] for v in range(VARS)], axis=1))
    given[:local, :] = high
    given[local:, :] = low

    @pl.when(s > 0)
    def _():
        elements = groups * local
        for k in range(FACES):
            match = jnp.where(iota((elements, local), 0) == up_v[k], 1.0, 0.0)
            hot[k * local:(k + 1) * local, :] = jnp.transpose(match).astype(BF16)
            wide_lift[k] = jnp.concatenate([lift_v[k]] * VARS, axis=1)
        jac = jnp.transpose(jac_v[...].reshape(FACES * VARS * VARS, local))
        place = iota((local, BLOCK), 1) >> 6
        for k in range(FACES):
            for v in range(VARS):
                total = jnp.zeros((local, BLOCK), F32)
                for w in range(VARS):
                    at = (k * VARS + w) * VARS + v
                    total = jnp.where(place == w, jac[:, at:at + 1], total)
                coeff[k * VARS + v] = total

    def operator(e):
        return jnp.concatenate(
            [
                (wide_lift[n // VARS] * coeff[n, e:e + 1, :]).astype(BF16)
                for n in range(FACES * VARS)
            ],
            axis=0,
        )

    def pick(rows, product, e, before):
        return jnp.where(rows == e, product, before)

    def own_parts(block):
        product = times_transposed(given[...], block)
        return product[:local] + product[local:]

    def full_operators():
        solved = jnp.zeros((local, BLOCK), F32)
        for e in range(local):
            block = inv_v[e].astype(BF16)
            product = times_transposed(jnp.concatenate([operator(e), given[...]], axis=0), block)
            full[e] = product[:USED].astype(BF16)
            solved = pick(row, product[USED:USED + local] + product[USED + local:], e, solved)
        base[...] = solved

    def send_copies():
        return [
            pltpu.make_async_remote_copy(
                src_ref=outgoing,
                dst_ref=incoming.at[pl.ds(pl.multiple_of(g * local, local), local), :],
                send_sem=send_sem.at[other],
                recv_sem=recv_sem.at[g],
                device_id={"chain": s + 1, "group": other},
                device_id_type=MESH,
            )
            for other in range(groups)
        ]

    def store(solved):
        for v in range(VARS):
            out_v[v] = solved[:, v * NODES:(v + 1) * NODES]

    def send(traces):
        outgoing[...] = traces.astype(BF16)
        pl.semaphore_wait(barrier, groups)
        for copy in send_copies():
            copy.start()

    def gathered():
        for other in range(groups):
            pltpu.make_async_remote_copy(
                src_ref=outgoing,
                dst_ref=incoming.at[pl.ds(other * local, local), :],
                send_sem=send_sem.at[other],
                recv_sem=recv_sem.at[other],
                device_id={"chain": s - 1, "group": other},
                device_id_type=MESH,
            ).wait_recv()
        found = jnp.dot(hot[...], incoming[...], preferred_element_type=F32)
        lane = iota((local, WIDE), 1)
        mixed = jnp.where(
            lane < SIDE, found[:local], jnp.where(lane < 2 * SIDE, found[local:2 * local], found[2 * local:])
        )
        return mixed.astype(BF16)[:, :USED]

    def whole(u):
        coupling = jnp.zeros((local, BLOCK), F32)
        for e in range(local):
            coupling = pick(row, jnp.dot(u, full[e], preferred_element_type=F32), e, coupling)
        store(base[...] - coupling)

    @pl.when(s == 0)
    def _():
        solved = jnp.zeros((local, BLOCK), F32)
        for e in range(local):
            blocks[e].wait()
            solved = pick(row, own_parts(inv_v[e].astype(BF16)), e, solved)
        if chains > 1:
            send(jnp.dot(solved.astype(BF16), sel[...], preferred_element_type=F32))
        store(solved)

    @pl.when((s > 0) & (s < last))
    def _():
        solved = jnp.zeros((local, WIDE), F32)
        for e in range(local):
            blocks[e].wait()
            block = jnp.concatenate(
                [face_rows(inv_v.at[e]).astype(BF16), jnp.zeros((WIDE - USED, BLOCK), BF16)], axis=0
            )
            product = times_transposed(jnp.concatenate([operator(e), given[...]], axis=0), block)
            short[e] = product[:USED].astype(BF16)
            solved = pick(row_t, product[USED:USED + local] + product[USED + local:], e, solved)
        base_t[...] = solved

    @pl.when(s == last)
    def _():
        if chains > 1:
            for e in range(local):
                blocks[e].wait()

    @pl.when(s > 1)
    def _():
        full_operators()

    @pl.when((s > 0) & (s < last))
    def _():
        u = gathered()
        coupling = jnp.zeros((local, WIDE), F32)
        for e in range(local):
            coupling = pick(row_t, jnp.dot(u, short[e], preferred_element_type=F32), e, coupling)
        send(base_t[...] - coupling)

        @pl.when(s == 1)
        def _():
            full_operators()

        whole(u)

    @pl.when((s == last) & (s > 0))
    def _():
        if chains == 2:
            full_operators()
        whole(gathered())

    result = pltpu.make_async_copy(out_v, out_hbm.at[0], out_sem)
    result.start()

    @pl.when(s < last)
    def _():
        for copy in send_copies():
            copy.wait_send()

    result.wait()


def body(chains, groups, rhs, inv_block, flux_jac, up_elem, lift):
    local = rhs.shape[3]
    elements = groups * local
    anywhere = pl.BlockSpec(memory_space=pl.ANY)
    solved = pl.pallas_call(
        functools.partial(kernel, chains, groups, local),
        out_shape=jax.ShapeDtypeStruct((1, VARS, local, NODES), F32),
        in_specs=[anywhere] * 5,
        out_specs=anywhere,
        scratch_shapes=[
            pltpu.VMEM((VARS, local, NODES), F32),
            pltpu.VMEM((local, BLOCK, BLOCK), F32),
            pltpu.VMEM((FACES * VARS * VARS, 1, local), F32),
            pltpu.VMEM((FACES, 1, local), jnp.int32),
            pltpu.VMEM((FACES, FACE, NODES), F32),
            pltpu.VMEM((VARS, local, NODES), F32),
            pltpu.VMEM((BLOCK, WIDE), BF16),
            pltpu.VMEM((FACES, FACE, BLOCK), F32),
            pltpu.VMEM((FACES * VARS, local, BLOCK), F32),
            pltpu.VMEM((FACES * local, elements), BF16),
            pltpu.VMEM((2 * local, BLOCK), BF16),
            pltpu.VMEM((local, BLOCK), F32),
            pltpu.VMEM((local, WIDE), F32),
            pltpu.VMEM((local, USED, BLOCK), BF16),
            pltpu.VMEM((local, USED, WIDE), BF16),
            pltpu.VMEM((local, WIDE), BF16),
            pltpu.VMEM((elements, WIDE), BF16),
            pltpu.SemaphoreType.DMA((4,)),
            pltpu.SemaphoreType.DMA((local,)),
            pltpu.SemaphoreType.DMA,
            pltpu.SemaphoreType.DMA((groups,)),
            pltpu.SemaphoreType.DMA((groups,)),
        ],
        compiler_params=pltpu.CompilerParams(
            collective_id=0, has_side_effects=True, vmem_limit_bytes=58 * 1024 * 1024
        ),
    )(
        jnp.transpose(rhs, (0, 1, 3, 2)),
        inv_block,
        jnp.transpose(flux_jac, (1, 2, 3, 0, 4)).reshape(FACES * VARS * VARS, 1, local),
        jnp.transpose(up_elem, (1, 0, 2)),
        jnp.transpose(lift, (0, 2, 1)),
    )
    return jnp.transpose(solved, (0, 1, 3, 2))


def solution(mesh):
    return jax.shard_map(
        functools.partial(body, mesh.shape["chain"], mesh.shape["group"]),
        mesh=mesh,
        in_specs=(
            P(("parts", "chain"), None, None, "group"),
            P(("parts", "chain"), "group", None, None),
            P(("parts", "chain"), None, None, None, "group"),
            P(("parts", "chain"), None, "group"),
            P(),
        ),
        out_specs=P(("parts", "chain"), None, None, "group"),
        check_vma=False,
    )
```

```python
import functools

import jax
import jax.numpy as jnp
from jax import lax
from jax.experimental import pallas as pl
from jax.experimental.pallas import tpu as pltpu
from jax.sharding import PartitionSpec as P

VARS = 5
NODES = 64
FACE = 16
BLOCK = VARS * NODES
FACES = 3
SIDE = VARS * FACE
USED = FACES * SIDE
WIDE = 256
MESH = pl.DeviceIdType.MESH
F32 = jnp.float32
BF16 = jnp.bfloat16


def iota(shape, axis):
    return lax.broadcasted_iota(jnp.int32, shape, axis)


def select_operator():
    shape = (BLOCK, WIDE)
    col = iota(shape, 1)
    second, third = col >= SIDE, col >= 2 * SIDE
    rest = col - jnp.where(third, 2 * SIDE, jnp.where(second, SIDE, 0))
    f = rest & 15
    node = jnp.where(third, (f << 2) + 3, jnp.where(second, ((f >> 2) << 4) + 12 + (f & 3), 48 + f))
    wanted = jnp.where(col < USED, ((rest >> 4) << 6) + node, BLOCK)
    return jnp.where(iota(shape, 0) == wanted, 1.0, 0.0).astype(BF16)


def halves(x):
    high = x.astype(BF16)
    return high, (x - high.astype(F32)).astype(BF16)


def times_transposed(a, b):
    return lax.dot_general(a, b, (((1,), (1,)), ((), ())), preferred_element_type=F32)


def face_rows(block):
    rows = []
    cube = block[...]
    rows.append(cube.reshape(VARS, NODES, BLOCK)[:, NODES - FACE:, :].reshape(SIDE, BLOCK))
    rows.append(cube.reshape(VARS * 4, 16, BLOCK)[:, 12:, :].reshape(SIDE, BLOCK))
    rows.append(cube.reshape(SIDE, 4, BLOCK)[:, 3, :])
    return jnp.concatenate(rows, axis=0)


def kernel(chains, groups, local, rhs_hbm, inv_hbm, jac_hbm, up_hbm, lift_hbm, out_hbm,
           rhs_v, inv_v, jac_v, up_v, lift_v, out_v, sel, wide_lift, coeff, hot, given, base, base_t, kept, short,
           outgoing, incoming, small_sem, inv_sem, out_sem, send_sem, recv_sem):
    s = lax.axis_index("chain")
    g = lax.axis_index("group")
    last = chains - 1
    small = [
        pltpu.make_async_copy(src, dst, small_sem.at[n])
        for n, (src, dst) in enumerate(
            ((up_hbm, up_v), (jac_hbm, jac_v), (lift_hbm, lift_v), (rhs_hbm.at[0], rhs_v))
        )
    ]
    for copy in small:
        copy.start()
    blocks = [pltpu.make_async_copy(inv_hbm.at[0, e], inv_v.at[e], inv_sem.at[e]) for e in range(local)]
    for copy in blocks:
        copy.start()

    barrier = pltpu.get_barrier_semaphore()

    @pl.when(s > 0)
    def _():
        for other in range(groups):
            pl.semaphore_signal(
                barrier, inc=1, device_id={"chain": s - 1, "group": other}, device_id_type=MESH
            )

    row = iota((local, BLOCK), 0)
    row_t = iota((local, WIDE), 0)
    sel[...] = select_operator()
    for copy in small:
        copy.wait()
    high, low = halves(jnp.concatenate([rhs_v[v] for v in range(VARS)], axis=1))
    given[:local, :] = high
    given[local:, :] = low

    @pl.when(s > 0)
    def _():
        elements = groups * local
        for k in range(FACES):
            match = jnp.where(iota((elements, local), 0) == up_v[k], 1.0, 0.0)
            hot[k * local:(k + 1) * local, :] = jnp.transpose(match).astype(BF16)
            wide_lift[k] = jnp.concatenate([lift_v[k]] * VARS, axis=1)
        jac = jnp.transpose(jac_v[...].reshape(FACES * VARS * VARS, local))
        place = iota((local, BLOCK), 1) >> 6
        for k in range(FACES):
            for v in range(VARS):
                total = jnp.zeros((local, BLOCK), F32)
                for w in range(VARS):
                    at = (k * VARS + w) * VARS + v
                    total = jnp.where(place == w, jac[:, at:at + 1], total)
                coeff[k * VARS + v] = total

    def operator(e):
        return jnp.concatenate(
            [
                (wide_lift[n // VARS] * coeff[n, e:e + 1, :]).astype(BF16)
                for n in range(FACES * VARS)
            ],
            axis=0,
        )

    def pick(rows, product, e, before):
        return jnp.where(rows == e, product, before)

    def solve(right, arriving):
        high, low = halves(right)
        columns = jnp.transpose(
            jnp.concatenate([high.astype(F32), low.astype(F32)], axis=0)
        ).astype(BF16)
        lane = iota((BLOCK, 2 * local), 1)
        total = jnp.zeros((BLOCK, 2 * local), F32)
        for e in range(local):
            if arriving is not None:
                arriving[e].wait()
            block = inv_v[e].astype(BF16)
            product = jnp.dot(block, columns, preferred_element_type=F32)
            total = jnp.where((lane == e) | (lane == e + local), product, total)
        return jnp.transpose(total[:, :local] + total[:, local:])

    def full_operators():
        solved = jnp.zeros((local, BLOCK), F32)
        for e in range(local):
            blocks[e].wait()
            block = inv_v[e].astype(BF16)
            product = times_transposed(jnp.concatenate([operator(e), given[...]], axis=0), block)
            kept[e] = product[:USED].astype(BF16)
            solved = pick(row, product[USED:USED + local] + product[USED + local:], e, solved)
        base[...] = solved

    def send_copies():
        return [
            pltpu.make_async_remote_copy(
                src_ref=outgoing,
                dst_ref=incoming.at[pl.ds(pl.multiple_of(g * local, local), local), :],
                send_sem=send_sem.at[other],
                recv_sem=recv_sem.at[g],
                device_id={"chain": s + 1, "group": other},
                device_id_type=MESH,
            )
            for other in range(groups)
        ]

    def store(solved):
        for v in range(VARS):
            out_v[v] = solved[:, v * NODES:(v + 1) * NODES]

    def send(traces):
        outgoing[...] = traces.astype(BF16)
        pl.semaphore_wait(barrier, groups)
        for copy in send_copies():
            copy.start()

    def gathered():
        for other in range(groups):
            pltpu.make_async_remote_copy(
                src_ref=outgoing,
                dst_ref=incoming.at[pl.ds(other * local, local), :],
                send_sem=send_sem.at[other],
                recv_sem=recv_sem.at[other],
                device_id={"chain": s - 1, "group": other},
                device_id_type=MESH,
            ).wait_recv()
        found = jnp.dot(hot[...], incoming[...], preferred_element_type=F32)
        lane = iota((local, WIDE), 1)
        mixed = jnp.where(
            lane < SIDE, found[:local], jnp.where(lane < 2 * SIDE, found[local:2 * local], found[2 * local:])
        )
        return mixed.astype(BF16)[:, :USED]

    def coupled(u):
        coupling = jnp.zeros((local, BLOCK), F32)
        for e in range(local):
            coupling = pick(row, jnp.dot(u, kept[e], preferred_element_type=F32), e, coupling)
        return coupling

    def right_sides():
        return jnp.concatenate([rhs_v[v] for v in range(VARS)], axis=1)

    @pl.when(s == 0)
    def _():
        solved = solve(right_sides(), blocks)
        if chains > 1:
            send(jnp.dot(solved.astype(BF16), sel[...], preferred_element_type=F32))
        store(solved)

    @pl.when((s > 0) & (s < last))
    def _():
        solved = jnp.zeros((local, WIDE), F32)
        for e in range(local):
            blocks[e].wait()
            block = jnp.concatenate(
                [face_rows(inv_v.at[e]).astype(BF16), jnp.zeros((WIDE - USED, BLOCK), BF16)], axis=0
            )
            own = operator(e)
            kept[e] = own
            product = times_transposed(jnp.concatenate([own, given[...]], axis=0), block)
            short[e] = product[:USED].astype(BF16)
            solved = pick(row_t, product[USED:USED + local] + product[USED + local:], e, solved)
        base_t[...] = solved
        u = gathered()
        coupling = jnp.zeros((local, WIDE), F32)
        for e in range(local):
            coupling = pick(row_t, jnp.dot(u, short[e], preferred_element_type=F32), e, coupling)
        send(base_t[...] - coupling)
        store(solve(right_sides() - coupled(u), None))

    @pl.when((s == last) & (s > 0))
    def _():
        full_operators()
        store(base[...] - coupled(gathered()))

    result = pltpu.make_async_copy(out_v, out_hbm.at[0], out_sem)
    result.start()

    @pl.when(s < last)
    def _():
        for copy in send_copies():
            copy.wait_send()

    result.wait()


def body(chains, groups, rhs, inv_block, flux_jac, up_elem, lift):
    local = rhs.shape[3]
    elements = groups * local
    anywhere = pl.BlockSpec(memory_space=pl.ANY)
    solved = pl.pallas_call(
        functools.partial(kernel, chains, groups, local),
        out_shape=jax.ShapeDtypeStruct((1, VARS, local, NODES), F32),
        in_specs=[anywhere] * 5,
        out_specs=anywhere,
        scratch_shapes=[
            pltpu.VMEM((VARS, local, NODES), F32),
            pltpu.VMEM((local, BLOCK, BLOCK), F32),
            pltpu.VMEM((FACES * VARS * VARS, 1, local), F32),
            pltpu.VMEM((FACES, 1, local), jnp.int32),
            pltpu.VMEM((FACES, FACE, NODES), F32),
            pltpu.VMEM((VARS, local, NODES), F32),
            pltpu.VMEM((BLOCK, WIDE), BF16),
            pltpu.VMEM((FACES, FACE, BLOCK), F32),
            pltpu.VMEM((FACES * VARS, local, BLOCK), F32),
            pltpu.VMEM((FACES * local, elements), BF16),
            pltpu.VMEM((2 * local, BLOCK), BF16),
            pltpu.VMEM((local, BLOCK), F32),
            pltpu.VMEM((local, WIDE), F32),
            pltpu.VMEM((local, USED, BLOCK), BF16),
            pltpu.VMEM((local, USED, WIDE), BF16),
            pltpu.VMEM((local, WIDE), BF16),
            pltpu.VMEM((elements, WIDE), BF16),
            pltpu.SemaphoreType.DMA((4,)),
            pltpu.SemaphoreType.DMA((local,)),
            pltpu.SemaphoreType.DMA,
            pltpu.SemaphoreType.DMA((groups,)),
            pltpu.SemaphoreType.DMA((groups,)),
        ],
        compiler_params=pltpu.CompilerParams(
            collective_id=0, has_side_effects=True, vmem_limit_bytes=58 * 1024 * 1024
        ),
    )(
        jnp.transpose(rhs, (0, 1, 3, 2)),
        inv_block,
        jnp.transpose(flux_jac, (1, 2, 3, 0, 4)).reshape(FACES * VARS * VARS, 1, local),
        jnp.transpose(up_elem, (1, 0, 2)),
        jnp.transpose(lift, (0, 2, 1)),
    )
    return jnp.transpose(solved, (0, 1, 3, 2))


def solution(mesh):
    return jax.shard_map(
        functools.partial(body, mesh.shape["chain"], mesh.shape["group"]),
        mesh=mesh,
        in_specs=(
            P(("parts", "chain"), None, None, "group"),
            P(("parts", "chain"), "group", None, None),
            P(("parts", "chain"), None, None, None, "group"),
            P(("parts", "chain"), None, "group"),
            P(),
        ),
        out_specs=P(("parts", "chain"), None, None, "group"),
        check_vma=False,
    )
```

```python
import functools

import jax
import jax.numpy as jnp
from jax import lax
from jax.experimental import pallas as pl
from jax.experimental.pallas import tpu as pltpu
from jax.sharding import PartitionSpec as P

VARS = 5
NODES = 64
FACE = 16
BLOCK = VARS * NODES
FACES = 3
SIDE = VARS * FACE
USED = FACES * SIDE
WIDE = 256
BATCH = 4
MESH = pl.DeviceIdType.MESH
F32 = jnp.float32
BF16 = jnp.bfloat16


def iota(shape, axis):
    return lax.broadcasted_iota(jnp.int32, shape, axis)


def select_operator():
    shape = (BLOCK, WIDE)
    col = iota(shape, 1)
    second, third = col >= SIDE, col >= 2 * SIDE
    rest = col - jnp.where(third, 2 * SIDE, jnp.where(second, SIDE, 0))
    f = rest & 15
    node = jnp.where(third, (f << 2) + 3, jnp.where(second, ((f >> 2) << 4) + 12 + (f & 3), 48 + f))
    wanted = jnp.where(col < USED, ((rest >> 4) << 6) + node, BLOCK)
    return jnp.where(iota(shape, 0) == wanted, 1.0, 0.0).astype(BF16)


def halves(x):
    high = x.astype(BF16)
    return high, (x - high.astype(F32)).astype(BF16)


def times_transposed(a, b):
    return lax.dot_general(a, b, (((1,), (1,)), ((), ())), preferred_element_type=F32)


def face_rows(block):
    rows = []
    cube = block[...]
    rows.append(cube.reshape(VARS, NODES, BLOCK)[:, NODES - FACE:, :].reshape(SIDE, BLOCK))
    rows.append(cube.reshape(VARS * 4, 16, BLOCK)[:, 12:, :].reshape(SIDE, BLOCK))
    rows.append(cube.reshape(SIDE, 4, BLOCK)[:, 3, :])
    return jnp.concatenate(rows, axis=0)


def kernel(chains, groups, local, rhs_hbm, inv_hbm, jac_hbm, up_hbm, lift_hbm, out_hbm,
           rhs_v, inv_v, jac_v, up_v, lift_v, out_v, sel, wide_lift, coeff, hot, given, base, base_t, kept, short,
           outgoing, incoming, small_sem, inv_sem, out_sem, send_sem, recv_sem):
    s = lax.axis_index("chain")
    g = lax.axis_index("group")
    last = chains - 1
    small = [
        pltpu.make_async_copy(src, dst, small_sem.at[n])
        for n, (src, dst) in enumerate(
            ((up_hbm, up_v), (jac_hbm, jac_v), (lift_hbm, lift_v), (rhs_hbm.at[0], rhs_v))
        )
    ]
    for copy in small:
        copy.start()
    blocks = [pltpu.make_async_copy(inv_hbm.at[0, e], inv_v.at[e], inv_sem.at[e]) for e in range(local)]
    for copy in blocks:
        copy.start()

    barrier = pltpu.get_barrier_semaphore()

    @pl.when(s > 0)
    def _():
        for other in range(groups):
            pl.semaphore_signal(
                barrier, inc=1, device_id={"chain": s - 1, "group": other}, device_id_type=MESH
            )

    row = iota((local, BLOCK), 0)
    row_t = iota((local, WIDE), 0)
    sel[...] = select_operator()
    for copy in small:
        copy.wait()
    high, low = halves(jnp.concatenate([rhs_v[v] for v in range(VARS)], axis=1))
    given[:local, :] = high
    given[local:, :] = low

    @pl.when(s > 0)
    def _():
        elements = groups * local
        for k in range(FACES):
            match = jnp.where(iota((elements, local), 0) == up_v[k], 1.0, 0.0)
            hot[k * local:(k + 1) * local, :] = jnp.transpose(match).astype(BF16)
            wide_lift[k] = jnp.concatenate([lift_v[k]] * VARS, axis=1)
        jac = jnp.transpose(jac_v[...].reshape(FACES * VARS * VARS, local))
        place = iota((local, BLOCK), 1) >> 6
        for k in range(FACES):
            for v in range(VARS):
                total = jnp.zeros((local, BLOCK), F32)
                for w in range(VARS):
                    at = (k * VARS + w) * VARS + v
                    total = jnp.where(place == w, jac[:, at:at + 1], total)
                coeff[k * VARS + v] = total

    def operator(e):
        return jnp.concatenate(
            [
                (wide_lift[n // VARS] * coeff[n, e:e + 1, :]).astype(BF16)
                for n in range(FACES * VARS)
            ],
            axis=0,
        )

    def arrive(e):
        if e % BATCH == 0:
            for block in blocks[e:e + BATCH]:
                block.wait()

    def pick(rows, product, e, before):
        return jnp.where(rows == e, product, before)

    def solve(right):
        high, low = halves(right)
        columns = jnp.transpose(
            jnp.concatenate([high.astype(F32), low.astype(F32)], axis=0)
        ).astype(BF16)
        lane = iota((BLOCK, 2 * local), 1)
        total = jnp.zeros((BLOCK, 2 * local), F32)
        for e in range(local):
            block = inv_v[e].astype(BF16)
            product = jnp.dot(block, columns, preferred_element_type=F32)
            total = jnp.where((lane == e) | (lane == e + local), product, total)
        return jnp.transpose(total[:, :local] + total[:, local:])

    def full_operators():
        solved = jnp.zeros((local, BLOCK), F32)
        for e in range(local):
            arrive(e)
            block = inv_v[e].astype(BF16)
            product = times_transposed(jnp.concatenate([operator(e), given[...]], axis=0), block)
            kept[e] = product[:USED].astype(BF16)
            solved = pick(row, product[USED:USED + local] + product[USED + local:], e, solved)
        base[...] = solved

    def send_copies():
        return [
            pltpu.make_async_remote_copy(
                src_ref=outgoing,
                dst_ref=incoming.at[pl.ds(pl.multiple_of(g * local, local), local), :],
                send_sem=send_sem.at[other],
                recv_sem=recv_sem.at[g],
                device_id={"chain": s + 1, "group": other},
                device_id_type=MESH,
            )
            for other in range(groups)
        ]

    def store(solved):
        for v in range(VARS):
            out_v[v] = solved[:, v * NODES:(v + 1) * NODES]

    def send(traces):
        outgoing[...] = traces.astype(BF16)
        pl.semaphore_wait(barrier, groups)
        for copy in send_copies():
            copy.start()

    def gathered():
        for other in range(groups):
            pltpu.make_async_remote_copy(
                src_ref=outgoing,
                dst_ref=incoming.at[pl.ds(other * local, local), :],
                send_sem=send_sem.at[other],
                recv_sem=recv_sem.at[other],
                device_id={"chain": s - 1, "group": other},
                device_id_type=MESH,
            ).wait_recv()
        found = jnp.dot(hot[...], incoming[...], preferred_element_type=F32)
        lane = iota((local, WIDE), 1)
        mixed = jnp.where(
            lane < SIDE, found[:local], jnp.where(lane < 2 * SIDE, found[local:2 * local], found[2 * local:])
        )
        return mixed.astype(BF16)[:, :USED]

    def coupled(u):
        coupling = jnp.zeros((local, BLOCK), F32)
        for e in range(local):
            coupling = pick(row, jnp.dot(u, kept[e], preferred_element_type=F32), e, coupling)
        return coupling

    def right_sides():
        return jnp.concatenate([rhs_v[v] for v in range(VARS)], axis=1)

    @pl.when(s == 0)
    def _():
        solved = jnp.zeros((local, BLOCK), F32)
        for e in range(local):
            arrive(e)
            product = times_transposed(given[...], inv_v[e].astype(BF16))
            solved = pick(row, product[:local] + product[local:], e, solved)
        if chains > 1:
            send(jnp.dot(solved.astype(BF16), sel[...], preferred_element_type=F32))
        store(solved)

    @pl.when((s > 0) & (s < last))
    def _():
        solved = jnp.zeros((local, WIDE), F32)
        for e in range(local):
            arrive(e)
            block = jnp.concatenate(
                [face_rows(inv_v.at[e]).astype(BF16), jnp.zeros((WIDE - USED, BLOCK), BF16)], axis=0
            )
            own = operator(e)
            kept[e] = own
            product = times_transposed(jnp.concatenate([own, given[...]], axis=0), block)
            short[e] = product[:USED].astype(BF16)
            solved = pick(row_t, product[USED:USED + local] + product[USED + local:], e, solved)
        base_t[...] = solved
        u = gathered()
        coupling = jnp.zeros((local, WIDE), F32)
        for e in range(local):
            coupling = pick(row_t, jnp.dot(u, short[e], preferred_element_type=F32), e, coupling)
        send(base_t[...] - coupling)
        store(solve(right_sides() - coupled(u)))

    @pl.when((s == last) & (s > 0))
    def _():
        full_operators()
        store(base[...] - coupled(gathered()))

    result = pltpu.make_async_copy(out_v, out_hbm.at[0], out_sem)
    result.start()

    @pl.when(s < last)
    def _():
        for copy in send_copies():
            copy.wait_send()

    result.wait()


def body(chains, groups, rhs, inv_block, flux_jac, up_elem, lift):
    local = rhs.shape[3]
    elements = groups * local
    anywhere = pl.BlockSpec(memory_space=pl.ANY)
    solved = pl.pallas_call(
        functools.partial(kernel, chains, groups, local),
        out_shape=jax.ShapeDtypeStruct((1, VARS, local, NODES), F32),
        in_specs=[anywhere] * 5,
        out_specs=anywhere,
        scratch_shapes=[
            pltpu.VMEM((VARS, local, NODES), F32),
            pltpu.VMEM((local, BLOCK, BLOCK), F32),
            pltpu.VMEM((FACES * VARS * VARS, 1, local), F32),
            pltpu.VMEM((FACES, 1, local), jnp.int32),
            pltpu.VMEM((FACES, FACE, NODES), F32),
            pltpu.VMEM((VARS, local, NODES), F32),
            pltpu.VMEM((BLOCK, WIDE), BF16),
            pltpu.VMEM((FACES, FACE, BLOCK), F32),
            pltpu.VMEM((FACES * VARS, local, BLOCK), F32),
            pltpu.VMEM((FACES * local, elements), BF16),
            pltpu.VMEM((2 * local, BLOCK), BF16),
            pltpu.VMEM((local, BLOCK), F32),
            pltpu.VMEM((local, WIDE), F32),
            pltpu.VMEM((local, USED, BLOCK), BF16),
            pltpu.VMEM((local, USED, WIDE), BF16),
            pltpu.VMEM((local, WIDE), BF16),
            pltpu.VMEM((elements, WIDE), BF16),
            pltpu.SemaphoreType.DMA((4,)),
            pltpu.SemaphoreType.DMA((local,)),
            pltpu.SemaphoreType.DMA,
            pltpu.SemaphoreType.DMA((groups,)),
            pltpu.SemaphoreType.DMA((groups,)),
        ],
        compiler_params=pltpu.CompilerParams(
            collective_id=0, has_side_effects=True, vmem_limit_bytes=58 * 1024 * 1024
        ),
    )(
        jnp.transpose(rhs, (0, 1, 3, 2)),
        inv_block,
        jnp.transpose(flux_jac, (1, 2, 3, 0, 4)).reshape(FACES * VARS * VARS, 1, local),
        jnp.transpose(up_elem, (1, 0, 2)),
        jnp.transpose(lift, (0, 2, 1)),
    )
    return jnp.transpose(solved, (0, 1, 3, 2))


def solution(mesh):
    return jax.shard_map(
        functools.partial(body, mesh.shape["chain"], mesh.shape["group"]),
        mesh=mesh,
        in_specs=(
            P(("parts", "chain"), None, None, "group"),
            P(("parts", "chain"), "group", None, None),
            P(("parts", "chain"), None, None, None, "group"),
            P(("parts", "chain"), None, "group"),
            P(),
        ),
        out_specs=P(("parts", "chain"), None, None, "group"),
        check_vma=False,
    )
```

```python
import functools

import jax
import jax.numpy as jnp
from jax import lax
from jax.experimental import pallas as pl
from jax.experimental.pallas import tpu as pltpu
from jax.sharding import PartitionSpec as P

VARS = 5
NODES = 64
FACE = 16
BLOCK = VARS * NODES
FACES = 3
SIDE = VARS * FACE
USED = FACES * SIDE
WIDE = 256
FIRST_BATCH = 4
BATCH = 8
MESH = pl.DeviceIdType.MESH
F32 = jnp.float32
BF16 = jnp.bfloat16


def iota(shape, axis):
    return lax.broadcasted_iota(jnp.int32, shape, axis)


def select_operator():
    shape = (BLOCK, WIDE)
    col = iota(shape, 1)
    second, third = col >= SIDE, col >= 2 * SIDE
    rest = col - jnp.where(third, 2 * SIDE, jnp.where(second, SIDE, 0))
    f = rest & 15
    node = jnp.where(third, (f << 2) + 3, jnp.where(second, ((f >> 2) << 4) + 12 + (f & 3), 48 + f))
    wanted = jnp.where(col < USED, ((rest >> 4) << 6) + node, BLOCK)
    return jnp.where(iota(shape, 0) == wanted, 1.0, 0.0).astype(BF16)


def halves(x):
    high = x.astype(BF16)
    return high, (x - high.astype(F32)).astype(BF16)


def times_transposed(a, b):
    return lax.dot_general(a, b, (((1,), (1,)), ((), ())), preferred_element_type=F32)


def face_rows(block):
    rows = []
    cube = block[...]
    rows.append(cube.reshape(VARS, NODES, BLOCK)[:, NODES - FACE:, :].reshape(SIDE, BLOCK))
    rows.append(cube.reshape(VARS * 4, 16, BLOCK)[:, 12:, :].reshape(SIDE, BLOCK))
    rows.append(cube.reshape(SIDE, 4, BLOCK)[:, 3, :])
    return jnp.concatenate(rows, axis=0)


def kernel(chains, groups, local, rhs_hbm, inv_hbm, jac_hbm, up_hbm, lift_hbm, out_hbm,
           rhs_v, inv_v, jac_v, up_v, lift_v, out_v, sel, wide_lift, coeff, hot, given, base, base_t, kept, short,
           outgoing, incoming, small_sem, inv_sem, out_sem, send_sem, recv_sem):
    s = lax.axis_index("chain")
    g = lax.axis_index("group")
    last = chains - 1
    small = [
        pltpu.make_async_copy(src, dst, small_sem.at[n])
        for n, (src, dst) in enumerate(
            ((up_hbm, up_v), (jac_hbm, jac_v), (lift_hbm, lift_v), (rhs_hbm.at[0], rhs_v))
        )
    ]
    for copy in small:
        copy.start()
    blocks = [pltpu.make_async_copy(inv_hbm.at[0, e], inv_v.at[e], inv_sem.at[e]) for e in range(local)]
    for copy in blocks:
        copy.start()

    barrier = pltpu.get_barrier_semaphore()

    @pl.when(s > 0)
    def _():
        for other in range(groups):
            pl.semaphore_signal(
                barrier, inc=1, device_id={"chain": s - 1, "group": other}, device_id_type=MESH
            )

    row = iota((local, BLOCK), 0)
    row_t = iota((local, WIDE), 0)
    sel[...] = select_operator()
    for copy in small:
        copy.wait()
    high, low = halves(jnp.concatenate([rhs_v[v] for v in range(VARS)], axis=1))
    given[:local, :] = high
    given[local:, :] = low

    @pl.when(s > 0)
    def _():
        elements = groups * local
        for k in range(FACES):
            match = jnp.where(iota((elements, local), 0) == up_v[k], 1.0, 0.0)
            hot[k * local:(k + 1) * local, :] = jnp.transpose(match).astype(BF16)
            wide_lift[k] = jnp.concatenate([lift_v[k]] * VARS, axis=1)
        jac = jnp.transpose(jac_v[...].reshape(FACES * VARS * VARS, local))
        place = iota((local, BLOCK), 1) >> 6
        for k in range(FACES):
            for v in range(VARS):
                total = jnp.zeros((local, BLOCK), F32)
                for w in range(VARS):
                    at = (k * VARS + w) * VARS + v
                    total = jnp.where(place == w, jac[:, at:at + 1], total)
                coeff[k * VARS + v] = total

    def operator(e):
        return jnp.concatenate(
            [
                (wide_lift[n // VARS] * coeff[n, e:e + 1, :]).astype(BF16)
                for n in range(FACES * VARS)
            ],
            axis=0,
        )

    def arrive(e, batch):
        if e % batch == 0:
            for block in blocks[e:e + batch]:
                block.wait()

    def pick(rows, product, e, before):
        return jnp.where(rows == e, product, before)

    def solve(right):
        high, low = halves(right)
        columns = jnp.transpose(
            jnp.concatenate([high.astype(F32), low.astype(F32)], axis=0)
        ).astype(BF16)
        lane = iota((BLOCK, 2 * local), 1)
        total = jnp.zeros((BLOCK, 2 * local), F32)
        for e in range(local):
            block = inv_v[e].astype(BF16)
            product = jnp.dot(block, columns, preferred_element_type=F32)
            total = jnp.where((lane == e) | (lane == e + local), product, total)
        return jnp.transpose(total[:, :local] + total[:, local:])

    def full_operators():
        solved = jnp.zeros((local, BLOCK), F32)
        for e in range(local):
            arrive(e, BATCH)
            block = inv_v[e].astype(BF16)
            product = times_transposed(jnp.concatenate([operator(e), given[...]], axis=0), block)
            kept[e] = product[:USED].astype(BF16)
            solved = pick(row, product[USED:USED + local] + product[USED + local:], e, solved)
        base[...] = solved

    def send_copies():
        return [
            pltpu.make_async_remote_copy(
                src_ref=outgoing,
                dst_ref=incoming.at[pl.ds(pl.multiple_of(g * local, local), local), :],
                send_sem=send_sem.at[other],
                recv_sem=recv_sem.at[g],
                device_id={"chain": s + 1, "group": other},
                device_id_type=MESH,
            )
            for other in range(groups)
        ]

    def store(solved):
        for v in range(VARS):
            out_v[v] = solved[:, v * NODES:(v + 1) * NODES]

    def send(traces):
        outgoing[...] = traces.astype(BF16)
        pl.semaphore_wait(barrier, groups)
        for copy in send_copies():
            copy.start()

    def gathered():
        for other in range(groups):
            pltpu.make_async_remote_copy(
                src_ref=outgoing,
                dst_ref=incoming.at[pl.ds(other * local, local), :],
                send_sem=send_sem.at[other],
                recv_sem=recv_sem.at[other],
                device_id={"chain": s - 1, "group": other},
                device_id_type=MESH,
            ).wait_recv()
        found = jnp.dot(hot[...], incoming[...], preferred_element_type=F32)
        lane = iota((local, WIDE), 1)
        mixed = jnp.where(
            lane < SIDE, found[:local], jnp.where(lane < 2 * SIDE, found[local:2 * local], found[2 * local:])
        )
        return mixed.astype(BF16)[:, :USED]

    def coupled(u):
        coupling = jnp.zeros((local, BLOCK), F32)
        for e in range(local):
            coupling = pick(row, jnp.dot(u, kept[e], preferred_element_type=F32), e, coupling)
        return coupling

    def right_sides():
        return jnp.concatenate([rhs_v[v] for v in range(VARS)], axis=1)

    @pl.when(s == 0)
    def _():
        solved = jnp.zeros((local, BLOCK), F32)
        for e in range(local):
            arrive(e, FIRST_BATCH)
            product = times_transposed(given[...], inv_v[e].astype(BF16))
            solved = pick(row, product[:local] + product[local:], e, solved)
        if chains > 1:
            send(jnp.dot(solved.astype(BF16), sel[...], preferred_element_type=F32))
        store(solved)

    @pl.when((s > 0) & (s < last))
    def _():
        solved = jnp.zeros((local, WIDE), F32)
        for e in range(local):
            arrive(e, BATCH)
            block = jnp.concatenate(
                [face_rows(inv_v.at[e]).astype(BF16), jnp.zeros((WIDE - USED, BLOCK), BF16)], axis=0
            )
            own = operator(e)
            kept[e] = own
            product = times_transposed(jnp.concatenate([own, given[...]], axis=0), block)
            short[e] = product[:USED].astype(BF16)
            solved = pick(row_t, product[USED:USED + local] + product[USED + local:], e, solved)
        base_t[...] = solved
        u = gathered()
        coupling = jnp.zeros((local, WIDE), F32)
        for e in range(local):
            coupling = pick(row_t, jnp.dot(u, short[e], preferred_element_type=F32), e, coupling)
        send(base_t[...] - coupling)
        store(solve(right_sides() - coupled(u)))

    @pl.when((s == last) & (s > 0))
    def _():
        full_operators()
        store(base[...] - coupled(gathered()))

    result = pltpu.make_async_copy(out_v, out_hbm.at[0], out_sem)
    result.start()

    @pl.when(s < last)
    def _():
        for copy in send_copies():
            copy.wait_send()

    result.wait()


def body(chains, groups, rhs, inv_block, flux_jac, up_elem, lift):
    local = rhs.shape[3]
    elements = groups * local
    anywhere = pl.BlockSpec(memory_space=pl.ANY)
    solved = pl.pallas_call(
        functools.partial(kernel, chains, groups, local),
        out_shape=jax.ShapeDtypeStruct((1, VARS, local, NODES), F32),
        in_specs=[anywhere] * 5,
        out_specs=anywhere,
        scratch_shapes=[
            pltpu.VMEM((VARS, local, NODES), F32),
            pltpu.VMEM((local, BLOCK, BLOCK), F32),
            pltpu.VMEM((FACES * VARS * VARS, 1, local), F32),
            pltpu.VMEM((FACES, 1, local), jnp.int32),
            pltpu.VMEM((FACES, FACE, NODES), F32),
            pltpu.VMEM((VARS, local, NODES), F32),
            pltpu.VMEM((BLOCK, WIDE), BF16),
            pltpu.VMEM((FACES, FACE, BLOCK), F32),
            pltpu.VMEM((FACES * VARS, local, BLOCK), F32),
            pltpu.VMEM((FACES * local, elements), BF16),
            pltpu.VMEM((2 * local, BLOCK), BF16),
            pltpu.VMEM((local, BLOCK), F32),
            pltpu.VMEM((local, WIDE), F32),
            pltpu.VMEM((local, USED, BLOCK), BF16),
            pltpu.VMEM((local, USED, WIDE), BF16),
            pltpu.VMEM((local, WIDE), BF16),
            pltpu.VMEM((elements, WIDE), BF16),
            pltpu.SemaphoreType.DMA((4,)),
            pltpu.SemaphoreType.DMA((local,)),
            pltpu.SemaphoreType.DMA,
            pltpu.SemaphoreType.DMA((groups,)),
            pltpu.SemaphoreType.DMA((groups,)),
        ],
        compiler_params=pltpu.CompilerParams(
            collective_id=0, has_side_effects=True, vmem_limit_bytes=58 * 1024 * 1024
        ),
    )(
        jnp.transpose(rhs, (0, 1, 3, 2)),
        inv_block,
        jnp.transpose(flux_jac, (1, 2, 3, 0, 4)).reshape(FACES * VARS * VARS, 1, local),
        jnp.transpose(up_elem, (1, 0, 2)),
        jnp.transpose(lift, (0, 2, 1)),
    )
    return jnp.transpose(solved, (0, 1, 3, 2))


def solution(mesh):
    return jax.shard_map(
        functools.partial(body, mesh.shape["chain"], mesh.shape["group"]),
        mesh=mesh,
        in_specs=(
            P(("parts", "chain"), None, None, "group"),
            P(("parts", "chain"), "group", None, None),
            P(("parts", "chain"), None, None, None, "group"),
            P(("parts", "chain"), None, "group"),
            P(),
        ),
        out_specs=P(("parts", "chain"), None, None, "group"),
        check_vma=False,
    )
```
